256 devices in a mesh: group: 8 (over x, core), band: 32 (over z, y).
Axes of the slice: x: 4, y: 4, z: 8, core: 2. Of those that a mesh axis runs over, the one named last changes fastest.
Arguments:
- base_latents: bfloat16 [2048, 32, 16, 128], P(('group', 'band')), may hold values from -41 to 41
- clip_lengths: int32 [8, 4], replicated, may hold values from 17 to 81, as said below
- clip_group: int32 [8, 4], replicated, may hold values from 0 to 7, as said below
- conv_weight: bfloat16 [3, 3, 128, 128], replicated, may hold values from -0.1875 to 0.1875
- w_qkv: bfloat16 [128, 384], replicated, may hold values from -0.5 to 0.5
- query_gain: float32 [128], replicated, may hold values from 0.5 to 90
- w_out: bfloat16 [128, 128], replicated, may hold values from -1.5 to 1.5
- w_up: bfloat16 [128, 512], replicated, may hold values from -0.5 to 0.5
- w_down: bfloat16 [512, 128], replicated, may hold values from -0.25 to 0.25
Outputs:
- refined: bfloat16 [8, 768, 32, 16, 128], P('group', 'band')
The draws below stay inside these ranges and needn't reach their ends.
Inputs may be any that keep to these rules, and one draw needn't show every extreme that they name: `clip_lengths`: row p lists the frame counts of base pool p's clips in the order of its frames; every row sums to 256 and holds one clip of exactly 81 frames. `clip_group`: the groups in one row are distinct, and one SR group receives a 81-frame clip from every pool.
All inputs are finite; a program needn't handle non-finite values.
Results may differ from the reference program's by a relative error of at most 0.013.
The reference program's roundings to bfloat16 on the way count: a program that leaves them out, or rounds other values in their place, can miss the bound.
Values may be sent and summed in bfloat16 or wider, within the bound.
No kernel may reach another device: no remote copies, remote signals or barrier semaphores. Data moves between devices by JAX's collectives and lax.ppermute only.
A program may use at most 64 MiB of HBM per device.

```python
import jax
import jax.numpy as jnp
from jax import lax

C = 128
HEADS = 8
HEAD_DIM = 16
FFH = 512
CLIPS = 4
LMAX = 81
LMIN = 17
POOL_FRAMES = 256
TH = 32
TW = 16
FRAMES = 2048
LPAD = 96
SLOTS = 768
N_GROUP = 8


def clip_plan(key):
    key_first, key_second, key_busy, key_rank, key_roll = jax.random.split(key, 5)
    remainder = POOL_FRAMES - LMAX
    first_len = jax.random.randint(key_first, (N_GROUP,), max(LMIN, remainder - 2 * LMAX), min(LMAX, remainder - 2 * LMIN) + 1)
    lower = jnp.maximum(LMIN, remainder - first_len - LMAX)
    upper = jnp.minimum(LMAX, remainder - first_len - LMIN)
    second_len = jax.random.randint(key_second, (N_GROUP,), lower, upper + 1)
    third_len = remainder - first_len - second_len
    longest = jnp.full((N_GROUP,), LMAX, jnp.int32)
    lengths = jnp.stack([longest, first_len, second_len, third_len], axis=1).astype(jnp.int32)
    busiest = jax.random.randint(key_busy, (), 0, N_GROUP)
    columns = jnp.arange(N_GROUP, dtype=jnp.int32)
    scores = jax.random.randint(key_rank, (N_GROUP, N_GROUP), 0, 1 << 20) * N_GROUP + columns[None, :]
    scores = jnp.where(columns[None, :] == busiest, -1, scores)
    ranked = jnp.argsort(scores, axis=1, stable=True)[:, :CLIPS].astype(jnp.int32)
    rotation = jax.random.randint(key_roll, (N_GROUP, 1), 0, CLIPS)
    placing = (jnp.arange(CLIPS, dtype=jnp.int32)[None, :] + rotation) % CLIPS
    return (jnp.take_along_axis(lengths, placing, axis=1), jnp.take_along_axis(ranked, placing, axis=1))


def draw_clip_lengths(key, part):
    lengths, groups = clip_plan(key)
    return lengths


def draw_clip_group(key, part):
    lengths, groups = clip_plan(key)
    return groups


def draw_base_latents(key, part):
    key = jax.random.fold_in(key, 5)
    key_values, key_channel, key_pixel = jax.random.split(key, 3)
    channel_scale = jnp.exp(jax.random.uniform(key_channel, (C,), jnp.float32, jnp.log(0.32), jnp.log(3.2)))
    pixel_scale = jnp.exp(jax.random.uniform(key_pixel, (FRAMES, TH, TW, 1), jnp.float32, jnp.log(0.32), jnp.log(3.2)))
    raw_values = jnp.clip(jax.random.normal(key_values, (FRAMES, TH, TW, C), jnp.float32), -4.0, 4.0)
    return (raw_values * channel_scale * pixel_scale).astype(jnp.bfloat16)


def draw_query_gain(key, part):
    key = jax.random.fold_in(key, 11)
    lower, upper = (0.5, 3.0)
    uniform_draw = jax.random.uniform(key, (C,), jnp.float32)
    return jnp.exp(jnp.log(lower) + uniform_draw * (jnp.log(upper) - jnp.log(lower)))


def normal_values(own_key, extent, width, reach, held_as=jnp.bfloat16):
    values = width * jax.random.normal(own_key, extent, jnp.float32)
    return jnp.clip(values, min=-reach, max=reach).astype(held_as)


def setup_inputs(seed: int = 0) -> dict:
    arg_keys = jax.random.split(jax.random.key(seed), 10)
    return {
        "base_latents": draw_base_latents(jax.random.fold_in(arg_keys[9], 71), 0),
        "clip_lengths": draw_clip_lengths(jax.random.fold_in(arg_keys[9], 71), 0),
        "clip_group": draw_clip_group(jax.random.fold_in(arg_keys[9], 71), 0),
        "conv_weight": normal_values(arg_keys[3], (3, 3, C, C), (9 * C) ** -0.5, 0.1875),
        "w_qkv": normal_values(arg_keys[4], (C, 3 * C), C ** -0.5, 0.5),
        "query_gain": draw_query_gain(jax.random.fold_in(arg_keys[9], 71), 0),
        "w_out": normal_values(arg_keys[6], (C, C), 0.35, 1.5),
        "w_up": normal_values(arg_keys[7], (C, FFH), C ** -0.5, 0.5),
        "w_down": normal_values(arg_keys[8], (FFH, C), FFH ** -0.5, 0.25),
    }


EPS = 1e-06

def rms_scale(values, reduce_axis):
    return values * lax.rsqrt(lax.optimization_barrier(jnp.mean(values * values, axis=reduce_axis, keepdims=True)) + EPS)

def round_through(tensor):
    return lax.optimization_barrier(tensor.astype(jnp.bfloat16)).astype(jnp.float32)

def conv_block(frames, conv_weight):
    latent_wide = frames.astype(jnp.float32)
    normed = jax.nn.silu(rms_scale(latent_wide, -1)).astype(jnp.bfloat16)
    convolved = lax.conv_general_dilated(normed.astype(jnp.float32), conv_weight.astype(jnp.float32), (1, 1), 'SAME', dimension_numbers=('NHWC', 'HWIO', 'NHWC'), precision=lax.Precision.HIGHEST)
    return (latent_wide + convolved).astype(jnp.bfloat16)

def temporal_block(tile_row, same_clip, w_qkv, query_gain, w_out, w_up, w_down):
    frames, pixels, channels = tile_row.shape
    slab_wide = tile_row.astype(jnp.float32).reshape(-1, channels)
    normed = rms_scale(slab_wide, -1).astype(jnp.bfloat16)
    projected = jnp.dot(normed, w_qkv, preferred_element_type=jnp.float32).astype(jnp.bfloat16)
    projected = projected.reshape(frames, pixels, 3, HEADS, HEAD_DIM)
    queries = rms_scale(projected[:, :, 0].astype(jnp.float32), -1) * query_gain.reshape(HEADS, HEAD_DIM)
    queries = round_through(queries)
    key_heads = round_through(rms_scale(projected[:, :, 1].astype(jnp.float32), -1))
    value_heads = projected[:, :, 2].astype(jnp.float32)
    scores = jnp.einsum('aphd,bphd->phab', queries, key_heads) * HEAD_DIM ** (-0.5)
    scores = jnp.where(same_clip[None, None], scores, -1e+30)
    row_top = lax.optimization_barrier(jnp.max(scores, axis=-1, keepdims=True))
    weights = jnp.exp(scores - row_top)
    weights = round_through(weights / lax.optimization_barrier(jnp.sum(weights, axis=-1, keepdims=True)))
    mixed = jnp.einsum('phab,bphd->aphd', weights, value_heads).astype(jnp.bfloat16)
    mixed = mixed.reshape(-1, channels)
    middle = (slab_wide + jnp.dot(mixed, w_out, preferred_element_type=jnp.float32)).astype(jnp.bfloat16)
    mlp_input = rms_scale(middle.astype(jnp.float32), -1).astype(jnp.bfloat16)
    lifted = jax.nn.silu(jnp.dot(mlp_input, w_up, preferred_element_type=jnp.float32)).astype(jnp.bfloat16)
    result = middle.astype(jnp.float32) + jnp.dot(lifted, w_down, preferred_element_type=jnp.float32)
    return result.astype(jnp.bfloat16).reshape(frames, pixels, channels)

def reference(base_latents, clip_lengths, clip_group, conv_weight, w_qkv, query_gain, w_out, w_up, w_down):
    pools = base_latents.reshape(N_GROUP, POOL_FRAMES, TH, TW, C)

    def per_pool(paired):
        frames, lengths = paired
        hidden = conv_block(frames, conv_weight)
        starts = jnp.cumsum(lengths) - lengths
        position = jnp.arange(POOL_FRAMES, dtype=jnp.int32)
        clip_of = lax.optimization_barrier(jnp.sum((position[:, None] >= starts[None, :]).astype(jnp.int32), axis=1))
        same_clip = clip_of[:, None] == clip_of[None, :]

        def per_row(tile_row):
            return temporal_block(tile_row, same_clip, w_qkv, query_gain, w_out, w_up, w_down)
        refined_rows = lax.map(per_row, hidden.transpose(1, 0, 2, 3))
        return refined_rows.transpose(1, 0, 2, 3)
    refined = lax.map(per_pool, (pools, clip_lengths))
    starts = jnp.cumsum(clip_lengths, axis=1) - clip_lengths
    slot_index = jnp.arange(LMAX, dtype=jnp.int32)

    def per_group(target_group):
        matched = clip_group == target_group
        seg_start = lax.optimization_barrier(jnp.sum(jnp.where(matched, starts, 0), axis=1))
        seg_len = lax.optimization_barrier(jnp.sum(jnp.where(matched, clip_lengths, 0), axis=1))
        live_slots = slot_index[None, :] < seg_len[:, None]
        picked = jnp.where(live_slots, seg_start[:, None] + slot_index[None, :], 0).astype(jnp.int32)
        chosen = jax.vmap(lambda tensor, rows_at: jnp.take(tensor, rows_at, axis=0))(refined, picked)
        chosen = jnp.where(live_slots[:, :, None, None, None], chosen, jnp.zeros((), jnp.bfloat16))
        padding = jnp.zeros((N_GROUP, LPAD - LMAX, TH, TW, C), jnp.bfloat16)
        chosen = jnp.concatenate([chosen, padding], axis=1)
        return chosen.transpose(1, 0, 2, 3, 4).reshape(SLOTS, TH, TW, C)
    return lax.map(per_group, jnp.arange(N_GROUP, dtype=jnp.int32))
```

```python
import functools

import jax
import jax.numpy as jnp
from jax import lax
from jax.experimental import pallas as pl
from jax.experimental.pallas import tpu as pltpu
from jax.sharding import PartitionSpec as P

HEADS = 8
HEAD_DIM = 16
LMAX = 81
EPS = 1e-6
C = 128
POOL = 256
REACH = 80
HALF = 128
KEYS = 208
FAR = -1e30
LOG2E = 1.4426950408889634
BF = jnp.bfloat16
F32 = jnp.float32


def square_parts(v):
    sq = v * v
    hi = sq.astype(BF)
    lo = (sq - hi.astype(F32)).astype(BF)
    return hi, lo


def attention_kernel(
    slots, starts, lens, x_ref, wk_ref, wqv_ref, gain_ref, wout_ref, wup_ref, wdown_ref, onehot_ref, far_ref,
    blockones_ref, out_ref, kaug, qbig, vaug, mixt, rows
):
    bands, flat, _ = x_ref.shape
    per_band = POOL // bands
    px = flat // per_band
    n2 = 2 * POOL
    kaug[:, C:] = onehot_ref[...]
    qbig[:C, :] = jnp.zeros((C, HEADS * n2), BF)
    qbig[C:, :] = far_ref[...]
    for pair in range(HEADS // 2):
        vaug[pair * 48 + 32 : pair * 48 + 48, :] = jnp.ones((16, n2), BF)

    def pixel_pair(pp, carry):
        both = x_ref[:, pl.ds(pl.multiple_of(pp * 16, 16), 16), :].astype(F32)
        xa = both[:, :per_band].reshape(POOL, C)
        xb = both[:, per_band:].reshape(POOL, C)
        x = jnp.concatenate([xa, xb], axis=0)
        n = (x * lax.rsqrt(jnp.mean(x * x, axis=-1, keepdims=True) + EPS)).astype(BF)
        k = jnp.dot(n, wk_ref[...], preferred_element_type=F32).astype(BF).astype(F32)
        ss = jnp.dot(
            jnp.concatenate(square_parts(k), axis=1), blockones_ref[...], preferred_element_type=F32
        )
        kaug[:, :C] = (k * lax.rsqrt(ss * (1.0 / HEAD_DIM) + EPS)).astype(BF)
        qv = lax.dot_general(
            wqv_ref[...], n, (((1,), (1,)), ((), ())), preferred_element_type=F32
        ).astype(BF)
        q = qv[:C].astype(F32).reshape(HEADS, HEAD_DIM, n2)
        qs = jnp.sum(q * q, axis=1, keepdims=True)
        q = (q * lax.rsqrt(qs * (1.0 / HEAD_DIM) + EPS)).reshape(C, n2) * gain_ref[...]
        q = q.astype(BF)
        for h in range(HEADS):
            head = slice(h * HEAD_DIM, (h + 1) * HEAD_DIM)
            for ib in range(4):
                lane = (ib * HEADS + h) * HALF
                qbig[head, lane : lane + HALF] = q[head, ib * HALF : (ib + 1) * HALF]
            pair, odd = h // 2, h % 2
            vaug[pair * 48 + odd * 16 : pair * 48 + odd * 16 + 16, :] = qv[C + h * HEAD_DIM : C + (h + 1) * HEAD_DIM]
        for i in range(2):
            for b in range(2):
                key0 = i * POOL + b * (POOL - KEYS)
                for pair in range(HEADS // 2):
                    lane = ((2 * i + b) * HEADS + 2 * pair) * HALF
                    s = jnp.dot(
                        kaug[key0 : key0 + KEYS, :],
                        qbig[:, lane : lane + 2 * HALF],
                        preferred_element_type=F32,
                    )
                    top = jnp.max(s, axis=0, keepdims=True)
                    e = jnp.exp2((s - top) * (LOG2E / 4)).astype(BF)
                    blank = jnp.zeros((POOL - KEYS, 2 * HALF), BF)
                    e = jnp.concatenate([e, blank] if b == 0 else [blank, e], axis=0)
                    o = jnp.dot(
                        vaug[pair * 48 : pair * 48 + 48, i * POOL : (i + 1) * POOL], e, preferred_element_type=F32
                    )
                    r = 1.0 / o[32:33]
                    lanes = slice(i * POOL + b * HALF, i * POOL + (b + 1) * HALF)
                    for odd in range(2):
                        part = o[odd * 16 : odd * 16 + 16, odd * HALF : (odd + 1) * HALF]
                        part = part * r[:, odd * HALF : (odd + 1) * HALF]
                        head = (2 * pair + odd) * HEAD_DIM
                        mixt[head : head + HEAD_DIM, lanes] = part.astype(BF)
        m = x + lax.dot_general(
            mixt[...], wout_ref[...], (((0,), (0,)), ((), ())), preferred_element_type=F32
        )
        m = m.astype(BF).astype(F32)
        n = (m * lax.rsqrt(jnp.mean(m * m, axis=-1, keepdims=True) + EPS)).astype(BF)
        up = jnp.dot(n, wup_ref[...], preferred_element_type=F32) * 0.5
        up = (up + up * jnp.tanh(up)).astype(BF)
        res = m + jnp.dot(up, wdown_ref[...], preferred_element_type=F32)
        for i in range(2):
            rows[pl.ds(2 * pp + i, POOL, stride=px), :] = res[i * POOL : (i + 1) * POOL]
        return carry

    lax.fori_loop(0, px // 2, pixel_pair, 0)

    clips = out_ref.shape[1] // slots

    def hand_out(b, carry):
        parts = []
        for c in range(clips):
            for jj in range(slots):
                j = b * slots + jj
                frame = jnp.minimum(starts[c] + j, POOL - 1)
                part = rows[pl.ds(pl.multiple_of(frame * px, px), px), :]
                parts.append(jnp.where(j < lens[c], part, 0.0))
        out_ref[b] = jnp.stack(parts, axis=0).astype(BF)
        return carry

    lax.fori_loop(0, bands, hand_out, 0)


def attention(x, starts, lens, w_qkv, query_gain, w_out, w_up, w_down, slots):
    bands, flat, _ = x.shape
    px = flat // (POOL // bands)
    n2 = 2 * POOL
    clips = starts.shape[0]
    frame = jnp.arange(POOL, dtype=jnp.int32)
    clip_of = jnp.sum((frame[:, None] >= starts[None, :]).astype(jnp.int32), axis=1) - 1
    lane = jnp.arange(C, dtype=jnp.int32)
    onehot = (clip_of[:, None] == lane[None, :]).astype(BF)
    onehot = jnp.concatenate([onehot, onehot], axis=0)
    apart = jnp.where((lane[:, None] < clips) & (lane[:, None] != clip_of[None, :]), FAR, 0.0).astype(BF)
    apart = jnp.broadcast_to(apart.reshape(C, 1, 2, 1, HALF), (C, 2, 2, HEADS, HALF)).reshape(C, HEADS * n2)
    blockones = (lane[:, None] // HEAD_DIM == lane[None, :] // HEAD_DIM).astype(BF)
    blockones = jnp.concatenate([blockones, blockones], axis=0)
    wqv = jnp.concatenate([w_qkv[:, :C].T, w_qkv[:, 2 * C :].T], axis=0)
    gain = jnp.broadcast_to(query_gain[:, None], (C, n2))
    vmem = pl.BlockSpec(memory_space=pltpu.VMEM)
    smem = pl.BlockSpec(memory_space=pltpu.SMEM)
    return pl.pallas_call(
        functools.partial(attention_kernel, slots),
        out_shape=jax.ShapeDtypeStruct((bands, clips * slots, px, C), BF),
        in_specs=[smem, smem] + [vmem] * 10,
        out_specs=vmem,
        scratch_shapes=[
            pltpu.VMEM((n2, 2 * C), BF),
            pltpu.VMEM((2 * C, HEADS * n2), BF),
            pltpu.VMEM((HEADS // 2 * 48, n2), BF),
            pltpu.VMEM((C, n2), BF),
            pltpu.VMEM((POOL * px, C), F32),
        ],
        compiler_params=pltpu.CompilerParams(vmem_limit_bytes=48 * 2**20),
        cost_estimate=pl.CostEstimate(
            flops=2 * POOL * px * C * 4000, bytes_accessed=4 * 2**20, transcendentals=POOL * px * HEADS * KEYS
        ),
        name="pool_attention",
    )(starts, lens, x, w_qkv[:, C : 2 * C], wqv, gain, w_out, w_up, w_down, onehot, apart, blockones)


CHUNKS = 2


def rms_scale(values, reduce_axis):
    return values * lax.rsqrt(jnp.mean(values * values, axis=reduce_axis, keepdims=True) + EPS)


def pack_kernel(slots, clip_of_group, y_ref, *out_refs):
    bands, _, px, _ = y_ref.shape
    groups = len(out_refs)
    for g in range(groups):
        c = clip_of_group[g]
        live = c >= 0
        for jj in range(slots):
            part = y_ref[:, jnp.maximum(c, 0) * slots + jj].astype(F32)
            part = jnp.where(live, part, 0.0).reshape(bands * px, C)
            out_refs[g][jj] = part.astype(BF)


def pack(y, clip_of_group, slots):
    groups = clip_of_group.shape[0]
    bands, _, px, _ = y.shape
    vmem = pl.BlockSpec(memory_space=pltpu.VMEM)
    return pl.pallas_call(
        functools.partial(pack_kernel, slots),
        out_shape=[jax.ShapeDtypeStruct((slots, bands * px, C), BF)] * groups,
        in_specs=[pl.BlockSpec(memory_space=pltpu.SMEM), vmem],
        out_specs=[vmem] * groups,
        compiler_params=pltpu.CompilerParams(vmem_limit_bytes=32 * 2**20),
        cost_estimate=pl.CostEstimate(flops=0, bytes_accessed=8 * 2**20, transcendentals=0),
        name="pack_slots",
    )(clip_of_group, y)


def place_kernel(groups, slots, chunks, me_ref, *refs):
    pieces, out_ref, sem = refs[: groups * chunks], refs[-2], refs[-1]
    chunk_px = pieces[0].shape[1]
    copies = []
    for chunk in range(chunks):
        for step in range(groups):
            source = lax.rem(me_ref[0] + groups - step, groups)
            for jj in range(slots):
                copies.append(
                    pltpu.make_async_copy(
                        pieces[chunk * groups + step].at[jj],
                        out_ref.at[jj * groups + source, pl.ds(chunk * chunk_px, chunk_px)],
                        sem.at[len(copies)],
                    )
                )
    for copy in copies:
        copy.start()
    for copy in copies:
        copy.wait()


def place(pieces, me, chunks):
    groups = len(pieces) // chunks
    slots, chunk_px, _ = pieces[0].shape
    vmem = pl.BlockSpec(memory_space=pltpu.VMEM)
    return pl.pallas_call(
        functools.partial(place_kernel, groups, slots, chunks),
        out_shape=jax.ShapeDtypeStruct((slots * groups, chunks * chunk_px, C), BF),
        in_specs=[pl.BlockSpec(memory_space=pltpu.SMEM)] + [vmem] * len(pieces),
        out_specs=pl.BlockSpec(memory_space=pl.ANY),
        scratch_shapes=[pltpu.SemaphoreType.DMA((len(pieces) * slots,))],
        compiler_params=pltpu.CompilerParams(vmem_limit_bytes=32 * 2**20),
        cost_estimate=pl.CostEstimate(flops=0, bytes_accessed=6 * 2**20, transcendentals=0),
        name="place_slots",
    )(me[None], *pieces)


def body(
    base_latents, clip_lengths, clip_group, conv_weight, w_qkv, query_gain, w_out, w_up, w_down
):
    groups = lax.axis_size("group")
    bands = lax.axis_size("band")
    frames_dev, tile_rows, tile_cols, channels = base_latents.shape
    latent_wide = base_latents.astype(jnp.float32)
    normed = jax.nn.silu(rms_scale(latent_wide, -1)).astype(jnp.bfloat16)
    convolved = lax.conv_general_dilated(
        normed,
        conv_weight,
        (1, 1),
        "SAME",
        dimension_numbers=("NHWC", "HWIO", "NHWC"),
        preferred_element_type=jnp.float32,
    )
    hidden = (latent_wide + convolved).astype(jnp.bfloat16)
    pixels = tile_rows * tile_cols
    px = pixels // bands // CHUNKS
    hidden = hidden.reshape(frames_dev, pixels, channels).transpose(1, 0, 2)
    hidden = hidden.reshape(CHUNKS, bands, px * frames_dev, channels)

    me = lax.axis_index("group")
    lengths = lax.dynamic_index_in_dim(clip_lengths, me, 0, keepdims=False)
    targets = lax.dynamic_index_in_dim(clip_group, me, 0, keepdims=False)
    starts = jnp.cumsum(lengths) - lengths
    slots = -(-LMAX // bands)
    aims = lax.rem(me + jnp.arange(groups, dtype=jnp.int32), groups)
    hit = targets[None, :] == aims[:, None]
    clip_of_group = jnp.where(
        jnp.any(hit, axis=1), jnp.argmax(hit, axis=1).astype(jnp.int32), -1
    )

    pieces = []
    for chunk in range(CHUNKS):
        pencil = lax.all_to_all(hidden[chunk], "band", split_axis=0, concat_axis=0, tiled=True)
        refined = attention(pencil, starts, lengths, w_qkv, query_gain, w_out, w_up, w_down, slots)
        arrived = lax.all_to_all(refined, "band", split_axis=0, concat_axis=0, tiled=True)
        packed = pack(arrived, clip_of_group, slots)
        for step in range(groups):
            ring = [(i, (i + step) % groups) for i in range(groups)]
            pieces.append(lax.ppermute(packed[step], "group", ring) if step else packed[step])
    placed = place(pieces, me, CHUNKS)
    return placed.reshape(1, slots * groups, tile_rows, tile_cols, channels)


def solution(mesh):
    placed = (P(("group", "band"), None, None, None), P(), P(), P(), P(), P(), P(), P(), P())
    return jax.shard_map(
        body,
        mesh=mesh,
        in_specs=placed,
        out_specs=P("group", "band", None, None, None),
        check_vma=False,
    )
```

```python
import functools

import jax
import jax.numpy as jnp
from jax import lax
from jax.experimental import pallas as pl
from jax.experimental.pallas import tpu as pltpu
from jax.sharding import PartitionSpec as P

HEADS = 8
HEAD_DIM = 16
LMAX = 81
EPS = 1e-6
C = 128
POOL = 256
REACH = 80
HALF = 128
KEYS = 208
FAR = -1e30
LOG2E = 1.4426950408889634
BF = jnp.bfloat16
F32 = jnp.float32


def square_parts(v):
    sq = v * v
    hi = sq.astype(BF)
    lo = (sq - hi.astype(F32)).astype(BF)
    return hi, lo


def attention_kernel(
    slots, starts, lens, x_ref, wqv_ref, wk_ref, gain_ref, wout_ref, wup_ref, wdown_ref, onehot_ref, far_ref,
    blockones_ref, out_ref, kaug, qbig, rows
):
    bands, flat, _ = x_ref.shape
    per_band = POOL // bands
    px = flat // per_band
    n2 = 2 * POOL
    lane = lax.broadcasted_iota(jnp.int32, (1, C), 1) // HEAD_DIM
    kaug[C:, :] = onehot_ref[...]
    for h in range(HEADS):
        qbig[h, :, C:] = far_ref[...]

    def pixel_pair(pp, carry):
        both = x_ref[:, pl.ds(pl.multiple_of(pp * 16, 16), 16), :].astype(F32)
        xa = both[:, :per_band].reshape(POOL, C)
        xb = both[:, per_band:].reshape(POOL, C)
        x = jnp.concatenate([xa, xb], axis=0)
        n = (x * lax.rsqrt(jnp.mean(x * x, axis=-1, keepdims=True) + EPS)).astype(BF)
        qv = jnp.dot(n, wqv_ref[...], preferred_element_type=F32).astype(BF)
        q = qv[:, :C].astype(F32)
        ss = jnp.dot(
            jnp.concatenate(square_parts(q), axis=1), blockones_ref[...], preferred_element_type=F32
        )
        q = q * lax.rsqrt(ss * (1.0 / HEAD_DIM) + EPS) * gain_ref[...]
        v = qv[:, C:]
        k = lax.dot_general(
            wk_ref[...], n, (((1,), (1,)), ((), ())), preferred_element_type=F32
        ).astype(BF)
        k = k.astype(F32).reshape(HEADS, HEAD_DIM, n2)
        ks = jnp.sum(k * k, axis=1, keepdims=True)
        kaug[:C, :] = (k * lax.rsqrt(ks * (1.0 / HEAD_DIM) + EPS)).reshape(C, n2).astype(BF)
        for h in range(HEADS):
            qbig[h, :, :C] = jnp.where(lane == h, q, 0.0).astype(BF)
        mixed = []
        for i in range(2):
            own = slice(i * POOL, (i + 1) * POOL)
            scores = jnp.dot(
                qbig[:, own, :].reshape(HEADS * POOL, 2 * C), kaug[:, own], preferred_element_type=F32
            )
            value_ones = jnp.concatenate([v[own], jnp.ones((POOL, C), BF)], axis=1)
            for h in range(HEADS):
                s = scores[h * POOL : (h + 1) * POOL]
                top = jnp.max(s, axis=-1, keepdims=True)
                e = jnp.exp2((s - top) * (LOG2E / 4)).astype(BF)
                o = jnp.dot(e, value_ones, preferred_element_type=F32)
                num = o[:, :C] if h == 0 else jnp.where(lane == h, o[:, :C], num)
                den = o[:, C:] if h == 0 else jnp.where(lane == h, o[:, C:], den)
            mixed.append((num / den).astype(BF))
        m = x + jnp.dot(
            jnp.concatenate(mixed, axis=0), wout_ref[...], preferred_element_type=F32
        )
        m = m.astype(BF).astype(F32)
        n = (m * lax.rsqrt(jnp.mean(m * m, axis=-1, keepdims=True) + EPS)).astype(BF)
        up = jnp.dot(n, wup_ref[...], preferred_element_type=F32) * 0.5
        up = (up + up * jnp.tanh(up)).astype(BF)
        res = m + jnp.dot(up, wdown_ref[...], preferred_element_type=F32)
        for i in range(2):
            rows[pl.ds(2 * pp + i, POOL, stride=px), :] = res[i * POOL : (i + 1) * POOL]
        return carry

    lax.fori_loop(0, px // 2, pixel_pair, 0)

    clips = out_ref.shape[1] // slots

    def hand_out(b, carry):
        parts = []
        for c in range(clips):
            for jj in range(slots):
                j = b * slots + jj
                frame = jnp.minimum(starts[c] + j, POOL - 1)
                part = rows[pl.ds(pl.multiple_of(frame * px, px), px), :]
                parts.append(jnp.where(j < lens[c], part, 0.0))
        out_ref[b] = jnp.stack(parts, axis=0).astype(BF)
        return carry

    lax.fori_loop(0, bands, hand_out, 0)


def attention(x, starts, lens, w_qkv, query_gain, w_out, w_up, w_down, slots):
    bands, flat, _ = x.shape
    px = flat // (POOL // bands)
    n2 = 2 * POOL
    clips = starts.shape[0]
    frame = jnp.arange(POOL, dtype=jnp.int32)
    clip_of = jnp.sum((frame[:, None] >= starts[None, :]).astype(jnp.int32), axis=1) - 1
    lane = jnp.arange(C, dtype=jnp.int32)
    onehot = (lane[:, None] == clip_of[None, :]).astype(BF)
    onehot = jnp.concatenate([onehot, onehot], axis=1)
    apart = jnp.where((lane[None, :] < clips) & (lane[None, :] != clip_of[:, None]), FAR, 0.0).astype(BF)
    apart = jnp.concatenate([apart, apart], axis=0)
    blockones = (lane[:, None] // HEAD_DIM == lane[None, :] // HEAD_DIM).astype(BF)
    blockones = jnp.concatenate([blockones, blockones], axis=0)
    wqv = jnp.concatenate([w_qkv[:, :C], w_qkv[:, 2 * C :]], axis=1)
    gain = query_gain.reshape(1, C)
    vmem = pl.BlockSpec(memory_space=pltpu.VMEM)
    smem = pl.BlockSpec(memory_space=pltpu.SMEM)
    return pl.pallas_call(
        functools.partial(attention_kernel, slots),
        out_shape=jax.ShapeDtypeStruct((bands, clips * slots, px, C), BF),
        in_specs=[smem, smem] + [vmem] * 10,
        out_specs=vmem,
        scratch_shapes=[
            pltpu.VMEM((2 * C, n2), BF),
            pltpu.VMEM((HEADS, n2, 2 * C), BF),
            pltpu.VMEM((POOL * px, C), F32),
        ],
        compiler_params=pltpu.CompilerParams(vmem_limit_bytes=48 * 2**20),
        cost_estimate=pl.CostEstimate(
            flops=2 * POOL * px * C * 4000, bytes_accessed=4 * 2**20, transcendentals=POOL * px * HEADS * KEYS
        ),
        name="pool_attention",
    )(starts, lens, x, wqv, w_qkv[:, C : 2 * C].T, gain, w_out, w_up, w_down, onehot, apart, blockones)


CHUNKS = 2


def rms_scale(values, reduce_axis):
    return values * lax.rsqrt(jnp.mean(values * values, axis=reduce_axis, keepdims=True) + EPS)


def conv_rows(latents, conv_weight, first, count):
    total = latents.shape[1]
    above, below = min(first, 1), min(total - first - count, 1)
    latent_wide = latents[:, first - above : first + count + below].astype(F32)
    normed = jax.nn.silu(rms_scale(latent_wide, -1)).astype(BF)
    convolved = lax.conv_general_dilated(
        normed,
        conv_weight,
        (1, 1),
        ((1 - above, 1 - below), (1, 1)),
        dimension_numbers=("NHWC", "HWIO", "NHWC"),
        preferred_element_type=F32,
    )
    return (latent_wide[:, above : above + count] + convolved).astype(BF)


def pack_kernel(slots, aims_of, clip_ref, y_ref, *out_refs):
    bands, _, px, _ = y_ref.shape
    for out_ref, aims in zip(out_refs, aims_of):
        for at, aim in enumerate(aims):
            c = clip_ref[aim]
            for jj in range(slots):
                part = y_ref[:, jnp.maximum(c, 0) * slots + jj].astype(F32)
                part = jnp.where(c >= 0, part, 0.0).reshape(bands * px, C)
                out_ref[at, jj] = part.astype(BF)


def pack(y, clip_of_aim, slots, aims_of):
    bands, _, px, _ = y.shape
    vmem = pl.BlockSpec(memory_space=pltpu.VMEM)
    return pl.pallas_call(
        functools.partial(pack_kernel, slots, aims_of),
        out_shape=[jax.ShapeDtypeStruct((len(aims), slots, bands * px, C), BF) for aims in aims_of],
        in_specs=[pl.BlockSpec(memory_space=pltpu.SMEM), vmem],
        out_specs=[vmem] * len(aims_of),
        compiler_params=pltpu.CompilerParams(vmem_limit_bytes=32 * 2**20),
        cost_estimate=pl.CostEstimate(flops=0, bytes_accessed=2 * 2**20, transcendentals=0),
        name="pack_slots",
    )(clip_of_aim, y)


def place_kernel(groups, slots, entries, me_ref, *refs):
    pieces, out_ref, sem = refs[:-2], refs[-2], refs[-1]
    chip, core = me_ref[0] // 2, lax.rem(me_ref[0], 2)
    copies = []
    for piece, at, chunk, hop, flip in entries:
        chunk_px = pieces[piece].shape[2]
        source = lax.rem(chip + groups // 2 - hop, groups // 2) * 2 + (1 - core if flip else core)
        for jj in range(slots):
            copies.append(
                pltpu.make_async_copy(
                    pieces[piece].at[at, jj],
                    out_ref.at[jj * groups + source, pl.ds(chunk * chunk_px, chunk_px)],
                    sem.at[len(copies)],
                )
            )
    for copy in copies:
        copy.start()
    for copy in copies:
        copy.wait()


def place(pieces, entries, me, groups, pixels):
    slots = pieces[0].shape[1]
    vmem = pl.BlockSpec(memory_space=pltpu.VMEM)
    return pl.pallas_call(
        functools.partial(place_kernel, groups, slots, entries),
        out_shape=jax.ShapeDtypeStruct((slots * groups, pixels, C), BF),
        in_specs=[pl.BlockSpec(memory_space=pltpu.SMEM)] + [vmem] * len(pieces),
        out_specs=pl.BlockSpec(memory_space=pl.ANY),
        scratch_shapes=[pltpu.SemaphoreType.DMA((len(entries) * slots,))],
        compiler_params=pltpu.CompilerParams(vmem_limit_bytes=32 * 2**20),
        cost_estimate=pl.CostEstimate(flops=0, bytes_accessed=6 * 2**20, transcendentals=0),
        name="place_slots",
    )(me[None], *pieces)


def to_chip(value, hop, flip, groups):
    pairs = [
        (chip * 2 + core, (chip + hop) % (groups // 2) * 2 + (core ^ flip))
        for chip in range(groups // 2)
        for core in range(2)
    ]
    return lax.ppermute(value, "group", pairs) if hop or flip else value


def body(
    base_latents, clip_lengths, clip_group, conv_weight, w_qkv, query_gain, w_out, w_up, w_down
):
    groups = lax.axis_size("group")
    bands = lax.axis_size("band")
    frames_dev, tile_rows, tile_cols, channels = base_latents.shape
    pixels = tile_rows * tile_cols
    px = pixels // bands // CHUNKS
    chunk_rows = tile_rows // CHUNKS

    me = lax.axis_index("group")
    lengths = lax.dynamic_index_in_dim(clip_lengths, me, 0, keepdims=False)
    targets = lax.dynamic_index_in_dim(clip_group, me, 0, keepdims=False)
    starts = jnp.cumsum(lengths) - lengths
    slots = -(-LMAX // bands)
    chips = groups // 2
    aim_list = [(hop, flip) for hop in range(chips) for flip in range(2)]
    aims = jnp.stack(
        [lax.rem(me // 2 + hop, chips) * 2 + lax.rem(me + flip, 2) for hop, flip in aim_list]
    )
    hit = targets[None, :] == aims[:, None]
    clip_index = jnp.arange(targets.shape[0], dtype=jnp.int32)
    clip_of_aim = jnp.max(jnp.where(hit, clip_index[None, :], -1), axis=1)

    pieces, entries = [], []
    for chunk in range(CHUNKS):
        hidden = conv_rows(base_latents, conv_weight, chunk * chunk_rows, chunk_rows)
        hidden = hidden.reshape(frames_dev, chunk_rows * tile_cols, channels).transpose(1, 0, 2)
        hidden = hidden.reshape(bands, px * frames_dev, channels)
        pencil = lax.all_to_all(hidden, "band", split_axis=0, concat_axis=0, tiled=True)
        refined = attention(pencil, starts, lengths, w_qkv, query_gain, w_out, w_up, w_down, slots)
        arrived = lax.all_to_all(refined, "band", split_axis=0, concat_axis=0, tiled=True)
        if chunk < CHUNKS - 1:
            packed = pack(
                arrived, clip_of_aim, slots, [[2 * hop, 2 * hop + 1] for hop in range(chips)]
            )
            landed = [to_chip(slab, hop, 0, groups) for hop, slab in enumerate(packed)]
            swapped = to_chip(jnp.stack([slab[1] for slab in landed]), 0, 1, groups)
            for hop, slab in enumerate(landed):
                entries += [(len(pieces), 0, chunk, hop, 0), (chips, hop, chunk, hop, 1)]
                pieces.append(slab)
            pieces.append(swapped)
        else:
            packed = pack(arrived, clip_of_aim, slots, [[i] for i in range(groups)])
            for (hop, flip), slab in zip(aim_list, packed):
                entries.append((len(pieces), 0, chunk, hop, flip))
                pieces.append(to_chip(slab, hop, flip, groups))
    placed = place(pieces, entries, me, groups, pixels)
    return placed.reshape(1, slots * groups, tile_rows, tile_cols, channels)


def solution(mesh):
    placed = (P(("group", "band"), None, None, None), P(), P(), P(), P(), P(), P(), P(), P())
    return jax.shard_map(
        body,
        mesh=mesh,
        in_specs=placed,
        out_specs=P("group", "band", None, None, None),
        check_vma=False,
    )
```

```python
import functools

import jax
import jax.numpy as jnp
from jax import lax
from jax.experimental import pallas as pl
from jax.experimental.pallas import tpu as pltpu
from jax.sharding import PartitionSpec as P

HEADS = 8
HEAD_DIM = 16
LMAX = 81
EPS = 1e-6
C = 128
POOL = 256
REACH = 80
HALF = 128
KEYS = 208
FAR = -1e30
LOG2E = 1.4426950408889634
BF = jnp.bfloat16
F32 = jnp.float32


def square_parts(v):
    sq = v * v
    hi = sq.astype(BF)
    lo = (sq - hi.astype(F32)).astype(BF)
    return hi, lo


def attention_kernel(
    slots, starts, lens, x_ref, wqv_ref, wk_ref, gain_ref, wout_ref, wup_ref, wdown_ref, onehot_ref, far_ref,
    blockones_ref, out_ref, kaug, qbig, rows
):
    bands, flat, _ = x_ref.shape
    per_band = POOL // bands
    px = flat // per_band
    n2 = 2 * POOL
    lane = lax.broadcasted_iota(jnp.int32, (1, C), 1) // HEAD_DIM
    kaug[C:, :] = onehot_ref[...]
    for h in range(HEADS):
        qbig[h, :, C:] = far_ref[...]

    def pixel_pair(pp, carry):
        both = x_ref[:, pl.ds(pl.multiple_of(pp * 16, 16), 16), :].astype(F32)
        xa = both[:, :per_band].reshape(POOL, C)
        xb = both[:, per_band:].reshape(POOL, C)
        x = jnp.concatenate([xa, xb], axis=0)
        n = (x * lax.rsqrt(jnp.mean(x * x, axis=-1, keepdims=True) + EPS)).astype(BF)
        qv = jnp.dot(n, wqv_ref[...], preferred_element_type=F32).astype(BF)
        q = qv[:, :C].astype(F32)
        ss = jnp.dot(
            jnp.concatenate(square_parts(q), axis=1), blockones_ref[...], preferred_element_type=F32
        )
        q = q * lax.rsqrt(ss * (1.0 / HEAD_DIM) + EPS) * gain_ref[...]
        v = qv[:, C:]
        k = lax.dot_general(
            wk_ref[...], n, (((1,), (1,)), ((), ())), preferred_element_type=F32
        ).astype(BF)
        k = k.astype(F32).reshape(HEADS, HEAD_DIM, n2)
        ks = jnp.sum(k * k, axis=1, keepdims=True)
        kaug[:C, :] = (k * lax.rsqrt(ks * (1.0 / HEAD_DIM) + EPS)).reshape(C, n2).astype(BF)
        for h in range(HEADS):
            qbig[h, :, :C] = jnp.where(lane == h, q, 0.0).astype(BF)
        mixed = []
        for i in range(2):
            own = slice(i * POOL, (i + 1) * POOL)
            scores = jnp.dot(
                qbig[:, own, :].reshape(HEADS * POOL, 2 * C), kaug[:, own], preferred_element_type=F32
            )
            value_ones = jnp.concatenate([v[own], jnp.ones((POOL, C), BF)], axis=1)
            for h in range(HEADS):
                s = scores[h * POOL : (h + 1) * POOL]
                top = jnp.max(s, axis=-1, keepdims=True)
                e = jnp.exp2((s - top) * (LOG2E / 4)).astype(BF)
                o = jnp.dot(e, value_ones, preferred_element_type=F32)
                num = o[:, :C] if h == 0 else jnp.where(lane == h, o[:, :C], num)
                den = o[:, C:] if h == 0 else jnp.where(lane == h, o[:, C:], den)
            mixed.append((num / den).astype(BF))
        m = x + jnp.dot(
            jnp.concatenate(mixed, axis=0), wout_ref[...], preferred_element_type=F32
        )
        m = m.astype(BF).astype(F32)
        n = (m * lax.rsqrt(jnp.mean(m * m, axis=-1, keepdims=True) + EPS)).astype(BF)
        up = jnp.dot(n, wup_ref[...], preferred_element_type=F32) * 0.5
        up = (up + up * jnp.tanh(up)).astype(BF)
        res = m + jnp.dot(up, wdown_ref[...], preferred_element_type=F32)
        for i in range(2):
            rows[pl.ds(2 * pp + i, POOL, stride=px), :] = res[i * POOL : (i + 1) * POOL]
        return carry

    lax.fori_loop(0, px // 2, pixel_pair, 0)

    clips = out_ref.shape[1] // slots

    def hand_out(b, carry):
        parts = []
        for c in range(clips):
            for jj in range(slots):
                j = b * slots + jj
                frame = jnp.minimum(starts[c] + j, POOL - 1)
                part = rows[pl.ds(pl.multiple_of(frame * px, px), px), :]
                parts.append(jnp.where(j < lens[c], part, 0.0))
        out_ref[b] = jnp.stack(parts, axis=0).astype(BF)
        return carry

    lax.fori_loop(0, bands, hand_out, 0)


def attention(x, starts, lens, w_qkv, query_gain, w_out, w_up, w_down, slots):
    bands, flat, _ = x.shape
    px = flat // (POOL // bands)
    n2 = 2 * POOL
    clips = starts.shape[0]
    frame = jnp.arange(POOL, dtype=jnp.int32)
    clip_of = jnp.sum((frame[:, None] >= starts[None, :]).astype(jnp.int32), axis=1) - 1
    lane = jnp.arange(C, dtype=jnp.int32)
    onehot = (lane[:, None] == clip_of[None, :]).astype(BF)
    onehot = jnp.concatenate([onehot, onehot], axis=1)
    apart = jnp.where((lane[None, :] < clips) & (lane[None, :] != clip_of[:, None]), FAR, 0.0).astype(BF)
    apart = jnp.concatenate([apart, apart], axis=0)
    blockones = (lane[:, None] // HEAD_DIM == lane[None, :] // HEAD_DIM).astype(BF)
    blockones = jnp.concatenate([blockones, blockones], axis=0)
    wqv = jnp.concatenate([w_qkv[:, :C], w_qkv[:, 2 * C :]], axis=1)
    gain = query_gain.reshape(1, C)
    vmem = pl.BlockSpec(memory_space=pltpu.VMEM)
    smem = pl.BlockSpec(memory_space=pltpu.SMEM)
    return pl.pallas_call(
        functools.partial(attention_kernel, slots),
        out_shape=jax.ShapeDtypeStruct((bands, clips * slots, px, C), BF),
        in_specs=[smem, smem] + [vmem] * 10,
        out_specs=vmem,
        scratch_shapes=[
            pltpu.VMEM((2 * C, n2), BF),
            pltpu.VMEM((HEADS, n2, 2 * C), BF),
            pltpu.VMEM((POOL * px, C), F32),
        ],
        compiler_params=pltpu.CompilerParams(vmem_limit_bytes=48 * 2**20),
        cost_estimate=pl.CostEstimate(
            flops=2 * POOL * px * C * 4000, bytes_accessed=4 * 2**20, transcendentals=POOL * px * HEADS * KEYS
        ),
        name="pool_attention",
    )(starts, lens, x, wqv, w_qkv[:, C : 2 * C].T, gain, w_out, w_up, w_down, onehot, apart, blockones)


CHUNKS = 2


def rms_scale(values, reduce_axis):
    return values * lax.rsqrt(jnp.mean(values * values, axis=reduce_axis, keepdims=True) + EPS)


def conv_rows(latents, conv_weight, first, count):
    total = latents.shape[1]
    above, below = min(first, 1), min(total - first - count, 1)
    latent_wide = latents[:, first - above : first + count + below].astype(F32)
    normed = jax.nn.silu(rms_scale(latent_wide, -1)).astype(BF)
    convolved = lax.conv_general_dilated(
        normed,
        conv_weight,
        (1, 1),
        ((1 - above, 1 - below), (1, 1)),
        dimension_numbers=("NHWC", "HWIO", "NHWC"),
        preferred_element_type=F32,
    )
    return (latent_wide[:, above : above + count] + convolved).astype(BF)


def pack_kernel(slots, aims_of, clip_ref, y_ref, *out_refs):
    bands, _, px, _ = y_ref.shape
    for out_ref, aims in zip(out_refs, aims_of):
        for at, aim in enumerate(aims):
            c = clip_ref[aim]
            for jj in range(slots):
                part = y_ref[:, jnp.maximum(c, 0) * slots + jj].astype(F32)
                part = jnp.where(c >= 0, part, 0.0).reshape(bands * px, C)
                out_ref[at, jj] = part.astype(BF)


def pack(y, clip_of_aim, slots, aims_of):
    bands, _, px, _ = y.shape
    vmem = pl.BlockSpec(memory_space=pltpu.VMEM)
    return pl.pallas_call(
        functools.partial(pack_kernel, slots, aims_of),
        out_shape=[jax.ShapeDtypeStruct((len(aims), slots, bands * px, C), BF) for aims in aims_of],
        in_specs=[pl.BlockSpec(memory_space=pltpu.SMEM), vmem],
        out_specs=[vmem] * len(aims_of),
        compiler_params=pltpu.CompilerParams(vmem_limit_bytes=32 * 2**20),
        cost_estimate=pl.CostEstimate(flops=0, bytes_accessed=2 * 2**20, transcendentals=0),
        name="pack_slots",
    )(clip_of_aim, y)


def place_kernel(groups, slots, entries, me_ref, *refs):
    pieces, out_ref, sem = refs[:-2], refs[-2], refs[-1]
    chip, core = me_ref[0] // 2, lax.rem(me_ref[0], 2)
    copies = []
    for piece, at, chunk, hop, flip in entries:
        chunk_px = pieces[piece].shape[2]
        source = lax.rem(chip + groups // 2 - hop, groups // 2) * 2 + (1 - core if flip else core)
        for jj in range(slots):
            copies.append(
                pltpu.make_async_copy(
                    pieces[piece].at[at, jj],
                    out_ref.at[jj * groups + source, pl.ds(chunk * chunk_px, chunk_px)],
                    sem.at[len(copies)],
                )
            )
    for copy in copies:
        copy.start()
    for copy in copies:
        copy.wait()


def place(pieces, entries, me, groups, pixels):
    slots = pieces[0].shape[1]
    vmem = pl.BlockSpec(memory_space=pltpu.VMEM)
    return pl.pallas_call(
        functools.partial(place_kernel, groups, slots, entries),
        out_shape=jax.ShapeDtypeStruct((slots * groups, pixels, C), BF),
        in_specs=[pl.BlockSpec(memory_space=pltpu.SMEM)] + [vmem] * len(pieces),
        out_specs=pl.BlockSpec(memory_space=pl.ANY),
        scratch_shapes=[pltpu.SemaphoreType.DMA((len(entries) * slots,))],
        compiler_params=pltpu.CompilerParams(vmem_limit_bytes=32 * 2**20),
        cost_estimate=pl.CostEstimate(flops=0, bytes_accessed=6 * 2**20, transcendentals=0),
        name="place_slots",
    )(me[None], *pieces)


def to_chip(value, hop, flip, groups):
    pairs = [
        (chip * 2 + core, (chip + hop) % (groups // 2) * 2 + (core ^ flip))
        for chip in range(groups // 2)
        for core in range(2)
    ]
    return lax.ppermute(value, "group", pairs) if hop or flip else value


def body(
    base_latents, clip_lengths, clip_group, conv_weight, w_qkv, query_gain, w_out, w_up, w_down
):
    groups = lax.axis_size("group")
    bands = lax.axis_size("band")
    frames_dev, tile_rows, tile_cols, channels = base_latents.shape
    pixels = tile_rows * tile_cols
    px = pixels // bands // CHUNKS
    chunk_rows = tile_rows // CHUNKS

    me = lax.axis_index("group")
    lengths = lax.dynamic_index_in_dim(clip_lengths, me, 0, keepdims=False)
    targets = lax.dynamic_index_in_dim(clip_group, me, 0, keepdims=False)
    starts = jnp.cumsum(lengths) - lengths
    slots = -(-LMAX // bands)
    chips = groups // 2
    aim_list = [(hop, flip) for hop in range(chips) for flip in range(2)]
    aims = jnp.stack(
        [lax.rem(me // 2 + hop, chips) * 2 + lax.rem(me + flip, 2) for hop, flip in aim_list]
    )
    hit = targets[None, :] == aims[:, None]
    clip_index = jnp.arange(targets.shape[0], dtype=jnp.int32)
    clip_of_aim = jnp.max(jnp.where(hit, clip_index[None, :], -1), axis=1)

    pieces, entries = [], []
    latents, to_swap = base_latents, []
    for chunk in range(CHUNKS):
        hidden = conv_rows(latents, conv_weight, chunk * chunk_rows, chunk_rows)
        latents, hidden = lax.optimization_barrier((latents, hidden))
        hidden = hidden.reshape(frames_dev, chunk_rows * tile_cols, channels).transpose(1, 0, 2)
        hidden = hidden.reshape(bands, px * frames_dev, channels)
        pencil = lax.all_to_all(hidden, "band", split_axis=0, concat_axis=0, tiled=True)
        refined = attention(pencil, starts, lengths, w_qkv, query_gain, w_out, w_up, w_down, slots)
        arrived = lax.all_to_all(refined, "band", split_axis=0, concat_axis=0, tiled=True)
        if chunk < CHUNKS - 1:
            packed = pack(
                arrived, clip_of_aim, slots, [[2 * hop, 2 * hop + 1] for hop in range(chips)]
            )
            for hop, slab in enumerate(packed):
                landed = to_chip(slab, hop, 0, groups)
                entries.append((len(pieces), 0, chunk, hop, 0))
                pieces.append(landed)
                to_swap.append((landed, chunk, hop))
        else:
            packed = pack(arrived, clip_of_aim, slots, [[i] for i in range(groups)])
            packed, landed = lax.optimization_barrier((packed, [slab for slab, _, _ in to_swap]))
            swapped = to_chip(jnp.stack([slab[1] for slab in landed]), 0, 1, groups)
            entries += [(len(pieces), at, of, hop, 1) for at, (_, of, hop) in enumerate(to_swap)]
            pieces.append(swapped)
            for (hop, flip), slab in zip(aim_list, packed):
                entries.append((len(pieces), 0, chunk, hop, flip))
                pieces.append(to_chip(slab, hop, flip, groups))
    placed = place(pieces, entries, me, groups, pixels)
    return placed.reshape(1, slots * groups, tile_rows, tile_cols, channels)


def solution(mesh):
    placed = (P(("group", "band"), None, None, None), P(), P(), P(), P(), P(), P(), P(), P())
    return jax.shard_map(
        body,
        mesh=mesh,
        in_specs=placed,
        out_specs=P("group", "band", None, None, None),
        check_vma=False,
    )
```

```python
import functools

import jax
import jax.numpy as jnp
from jax import lax
from jax.experimental import pallas as pl
from jax.experimental.pallas import tpu as pltpu
from jax.sharding import PartitionSpec as P

HEADS = 8
HEAD_DIM = 16
LMAX = 81
EPS = 1e-6
C = 128
POOL = 256
REACH = 80
HALF = 128
KEYS = 208
FAR = -1e30
LOG2E = 1.4426950408889634
BF = jnp.bfloat16
F32 = jnp.float32


def square_parts(v):
    sq = v * v
    hi = sq.astype(BF)
    lo = (sq - hi.astype(F32)).astype(BF)
    return hi, lo


def attention_kernel(
    slots, starts, lens, x_ref, wqv_ref, wk_ref, gain_ref, wout_ref, wup_ref, wdown_ref, onehot_ref, far_ref,
    blockones_ref, out_ref, kaug, qbig, rows
):
    bands, flat, _ = x_ref.shape
    per_band = POOL // bands
    px = flat // per_band
    n2 = 2 * POOL
    lane = lax.broadcasted_iota(jnp.int32, (1, C), 1) // HEAD_DIM
    kaug[C:, :] = onehot_ref[...]
    for h in range(HEADS):
        qbig[h, :, C:] = far_ref[...]

    def pixel_pair(pp, carry):
        both = x_ref[:, pl.ds(pl.multiple_of(pp * 16, 16), 16), :].astype(F32)
        xa = both[:, :per_band].reshape(POOL, C)
        xb = both[:, per_band:].reshape(POOL, C)
        x = jnp.concatenate([xa, xb], axis=0)
        n = (x * lax.rsqrt(jnp.mean(x * x, axis=-1, keepdims=True) + EPS)).astype(BF)
        qv = jnp.dot(n, wqv_ref[...], preferred_element_type=F32).astype(BF)
        q = qv[:, :C].astype(F32)
        ss = jnp.dot(
            jnp.concatenate(square_parts(q), axis=1), blockones_ref[...], preferred_element_type=F32
        )
        q = q * lax.rsqrt(ss * (1.0 / HEAD_DIM) + EPS) * gain_ref[...]
        v = qv[:, C:]
        k = lax.dot_general(
            wk_ref[...], n, (((1,), (1,)), ((), ())), preferred_element_type=F32
        ).astype(BF)
        k = k.astype(F32).reshape(HEADS, HEAD_DIM, n2)
        ks = jnp.sum(k * k, axis=1, keepdims=True)
        kaug[:C, :] = (k * lax.rsqrt(ks * (1.0 / HEAD_DIM) + EPS)).reshape(C, n2).astype(BF)
        for h in range(HEADS):
            qbig[h, :, :C] = jnp.where(lane == h, q, 0.0).astype(BF)
        mixed = []
        for i in range(2):
            own = slice(i * POOL, (i + 1) * POOL)
            scores = jnp.dot(
                qbig[:, own, :].reshape(HEADS * POOL, 2 * C), kaug[:, own], preferred_element_type=F32
            )
            value_ones = jnp.concatenate([v[own], jnp.ones((POOL, C), BF)], axis=1)
            for h in range(HEADS):
                s = scores[h * POOL : (h + 1) * POOL]
                top = jnp.max(s, axis=-1, keepdims=True)
                e = jnp.exp2((s - top) * (LOG2E / 4)).astype(BF)
                o = jnp.dot(e, value_ones, preferred_element_type=F32)
                num = o[:, :C] if h == 0 else jnp.where(lane == h, o[:, :C], num)
                den = o[:, C:] if h == 0 else jnp.where(lane == h, o[:, C:], den)
            mixed.append((num / den).astype(BF))
        m = x + jnp.dot(
            jnp.concatenate(mixed, axis=0), wout_ref[...], preferred_element_type=F32
        )
        m = m.astype(BF).astype(F32)
        n = (m * lax.rsqrt(jnp.mean(m * m, axis=-1, keepdims=True) + EPS)).astype(BF)
        up = jnp.dot(n, wup_ref[...], preferred_element_type=F32) * 0.5
        up = (up + up * jnp.tanh(up)).astype(BF)
        res = m + jnp.dot(up, wdown_ref[...], preferred_element_type=F32)
        for i in range(2):
            rows[pl.ds(2 * pp + i, POOL, stride=px), :] = res[i * POOL : (i + 1) * POOL]
        return carry

    lax.fori_loop(0, px // 2, pixel_pair, 0)

    clips = out_ref.shape[1] // slots

    def hand_out(b, carry):
        parts = []
        for c in range(clips):
            for jj in range(slots):
                j = b * slots + jj
                frame = jnp.minimum(starts[c] + j, POOL - 1)
                part = rows[pl.ds(pl.multiple_of(frame * px, px), px), :]
                parts.append(jnp.where(j < lens[c], part, 0.0))
        out_ref[b] = jnp.stack(parts, axis=0).astype(BF)
        return carry

    lax.fori_loop(0, bands, hand_out, 0)


def attention(x, starts, lens, w_qkv, query_gain, w_out, w_up, w_down, slots):
    bands, flat, _ = x.shape
    px = flat // (POOL // bands)
    n2 = 2 * POOL
    clips = starts.shape[0]
    frame = jnp.arange(POOL, dtype=jnp.int32)
    clip_of = jnp.sum((frame[:, None] >= starts[None, :]).astype(jnp.int32), axis=1) - 1
    lane = jnp.arange(C, dtype=jnp.int32)
    onehot = (lane[:, None] == clip_of[None, :]).astype(BF)
    onehot = jnp.concatenate([onehot, onehot], axis=1)
    apart = jnp.where((lane[None, :] < clips) & (lane[None, :] != clip_of[:, None]), FAR, 0.0).astype(BF)
    apart = jnp.concatenate([apart, apart], axis=0)
    blockones = (lane[:, None] // HEAD_DIM == lane[None, :] // HEAD_DIM).astype(BF)
    blockones = jnp.concatenate([blockones, blockones], axis=0)
    wqv = jnp.concatenate([w_qkv[:, :C], w_qkv[:, 2 * C :]], axis=1)
    gain = query_gain.reshape(1, C)
    vmem = pl.BlockSpec(memory_space=pltpu.VMEM)
    smem = pl.BlockSpec(memory_space=pltpu.SMEM)
    return pl.pallas_call(
        functools.partial(attention_kernel, slots),
        out_shape=jax.ShapeDtypeStruct((bands, clips * slots, px, C), BF),
        in_specs=[smem, smem] + [vmem] * 10,
        out_specs=vmem,
        scratch_shapes=[
            pltpu.VMEM((2 * C, n2), BF),
            pltpu.VMEM((HEADS, n2, 2 * C), BF),
            pltpu.VMEM((POOL * px, C), F32),
        ],
        compiler_params=pltpu.CompilerParams(vmem_limit_bytes=48 * 2**20),
        cost_estimate=pl.CostEstimate(
            flops=2 * POOL * px * C * 4000, bytes_accessed=4 * 2**20, transcendentals=POOL * px * HEADS * KEYS
        ),
        name="pool_attention",
    )(starts, lens, x, wqv, w_qkv[:, C : 2 * C].T, gain, w_out, w_up, w_down, onehot, apart, blockones)


CHUNKS = 2


def rms_scale(values, reduce_axis):
    return values * lax.rsqrt(jnp.mean(values * values, axis=reduce_axis, keepdims=True) + EPS)


def conv_rows(latents, conv_weight, first, count):
    total = latents.shape[1]
    above, below = min(first, 1), min(total - first - count, 1)
    latent_wide = latents[:, first - above : first + count + below].astype(F32)
    normed = jax.nn.silu(rms_scale(latent_wide, -1)).astype(BF)
    convolved = lax.conv_general_dilated(
        normed,
        conv_weight,
        (1, 1),
        ((1 - above, 1 - below), (1, 1)),
        dimension_numbers=("NHWC", "HWIO", "NHWC"),
        preferred_element_type=F32,
    )
    return (latent_wide[:, above : above + count] + convolved).astype(BF)


def pack_kernel(slots, aims_of, clip_ref, y_ref, *out_refs):
    bands, _, px, _ = y_ref.shape
    for out_ref, aims in zip(out_refs, aims_of):
        for at, aim in enumerate(aims):
            c = clip_ref[aim]
            for jj in range(slots):
                part = y_ref[:, jnp.maximum(c, 0) * slots + jj].astype(F32)
                part = jnp.where(c >= 0, part, 0.0).reshape(bands * px, C)
                out_ref[at, jj] = part.astype(BF)


def pack(y, clip_of_aim, slots, aims_of):
    bands, _, px, _ = y.shape
    vmem = pl.BlockSpec(memory_space=pltpu.VMEM)
    return pl.pallas_call(
        functools.partial(pack_kernel, slots, aims_of),
        out_shape=[jax.ShapeDtypeStruct((len(aims), slots, bands * px, C), BF) for aims in aims_of],
        in_specs=[pl.BlockSpec(memory_space=pltpu.SMEM), vmem],
        out_specs=[vmem] * len(aims_of),
        compiler_params=pltpu.CompilerParams(vmem_limit_bytes=32 * 2**20),
        cost_estimate=pl.CostEstimate(flops=0, bytes_accessed=2 * 2**20, transcendentals=0),
        name="pack_slots",
    )(clip_of_aim, y)


def place_kernel(groups, slots, entries, me_ref, *refs):
    pieces, out_ref, sem = refs[:-2], refs[-2], refs[-1]
    chip, core = me_ref[0] // 2, lax.rem(me_ref[0], 2)
    copies = []
    for piece, at, chunk, hop, flip in entries:
        chunk_px = pieces[piece].shape[2]
        source = lax.rem(chip + groups // 2 - hop, groups // 2) * 2 + (1 - core if flip else core)
        for jj in range(slots):
            copies.append(
                pltpu.make_async_copy(
                    pieces[piece].at[at, jj],
                    out_ref.at[jj * groups + source, pl.ds(chunk * chunk_px, chunk_px)],
                    sem.at[len(copies)],
                )
            )
    for copy in copies:
        copy.start()
    for copy in copies:
        copy.wait()


def place(pieces, entries, me, groups, pixels):
    slots = pieces[0].shape[1]
    vmem = pl.BlockSpec(memory_space=pltpu.VMEM)
    return pl.pallas_call(
        functools.partial(place_kernel, groups, slots, entries),
        out_shape=jax.ShapeDtypeStruct((slots * groups, pixels, C), BF),
        in_specs=[pl.BlockSpec(memory_space=pltpu.SMEM)] + [vmem] * len(pieces),
        out_specs=pl.BlockSpec(memory_space=pl.ANY),
        scratch_shapes=[pltpu.SemaphoreType.DMA((len(entries) * slots,))],
        compiler_params=pltpu.CompilerParams(vmem_limit_bytes=32 * 2**20),
        cost_estimate=pl.CostEstimate(flops=0, bytes_accessed=6 * 2**20, transcendentals=0),
        name="place_slots",
    )(me[None], *pieces)


def to_chip(value, hop, flip, groups):
    pairs = [
        (chip * 2 + core, (chip + hop) % (groups // 2) * 2 + (core ^ flip))
        for chip in range(groups // 2)
        for core in range(2)
    ]
    return lax.ppermute(value, "group", pairs) if hop or flip else value


def body(
    base_latents, clip_lengths, clip_group, conv_weight, w_qkv, query_gain, w_out, w_up, w_down
):
    groups = lax.axis_size("group")
    bands = lax.axis_size("band")
    frames_dev, tile_rows, tile_cols, channels = base_latents.shape
    pixels = tile_rows * tile_cols
    px = pixels // bands // CHUNKS
    chunk_rows = tile_rows // CHUNKS

    me = lax.axis_index("group")
    lengths = lax.dynamic_index_in_dim(clip_lengths, me, 0, keepdims=False)
    targets = lax.dynamic_index_in_dim(clip_group, me, 0, keepdims=False)
    starts = jnp.cumsum(lengths) - lengths
    slots = -(-LMAX // bands)
    chips = groups // 2
    aim_list = [(hop, flip) for hop in range(chips) for flip in range(2)]
    aims = jnp.stack(
        [lax.rem(me // 2 + hop, chips) * 2 + lax.rem(me + flip, 2) for hop, flip in aim_list]
    )
    hit = targets[None, :] == aims[:, None]
    clip_index = jnp.arange(targets.shape[0], dtype=jnp.int32)
    clip_of_aim = jnp.max(jnp.where(hit, clip_index[None, :], -1), axis=1)

    pieces, entries = [], []
    latents, to_swap = base_latents, []
    for chunk in range(CHUNKS):
        hidden = conv_rows(latents, conv_weight, chunk * chunk_rows, chunk_rows)
        latents, hidden = lax.optimization_barrier((latents, hidden))
        hidden = hidden.reshape(frames_dev, chunk_rows * tile_cols, channels).transpose(1, 0, 2)
        hidden = hidden.reshape(bands, px * frames_dev, channels)
        pencil = lax.all_to_all(hidden, "band", split_axis=0, concat_axis=0, tiled=True)
        refined = attention(pencil, starts, lengths, w_qkv, query_gain, w_out, w_up, w_down, slots)
        arrived = lax.all_to_all(refined, "band", split_axis=0, concat_axis=0, tiled=True)
        if chunk < CHUNKS - 1:
            packed = pack(
                arrived, clip_of_aim, slots, [[2 * hop, 2 * hop + 1] for hop in range(chips)]
            )
            for hop, slab in enumerate(packed):
                landed = to_chip(slab, hop, 0, groups)
                entries.append((len(pieces), 0, chunk, hop, 0))
                pieces.append(landed)
                to_swap.append((landed, chunk, hop))
        else:
            packed = pack(arrived, clip_of_aim, slots, [[i] for i in range(groups)])
            packed, landed = lax.optimization_barrier((packed, [slab for slab, _, _ in to_swap]))
            swapped = to_chip(jnp.stack([slab[1] for slab in landed]), 0, 1, groups)
            entries += [(len(pieces), at, of, hop, 1) for at, (_, of, hop) in enumerate(to_swap)]
            pieces.append(swapped)
            for hop, flip in ((2, 0), (1, 0), (3, 0), (2, 1), (1, 1), (3, 1), (0, 1), (0, 0)):
                entries.append((len(pieces), 0, chunk, hop, flip))
                pieces.append(to_chip(packed[aim_list.index((hop, flip))], hop, flip, groups))
    placed = place(pieces, entries, me, groups, pixels)
    return placed.reshape(1, slots * groups, tile_rows, tile_cols, channels)


def solution(mesh):
    placed = (P(("group", "band"), None, None, None), P(), P(), P(), P(), P(), P(), P(), P())
    return jax.shard_map(
        body,
        mesh=mesh,
        in_specs=placed,
        out_specs=P("group", "band", None, None, None),
        check_vma=False,
    )
```

```python
import functools

import jax
import jax.numpy as jnp
from jax import lax
from jax.experimental import pallas as pl
from jax.experimental.pallas import tpu as pltpu
from jax.sharding import PartitionSpec as P

HEADS = 8
HEAD_DIM = 16
LMAX = 81
EPS = 1e-6
C = 128
POOL = 256
REACH = 80
HALF = 128
KEYS = 208
FAR = -1e30
LOG2E = 1.4426950408889634
BF = jnp.bfloat16
F32 = jnp.float32


def square_parts(v):
    sq = v * v
    hi = sq.astype(BF)
    lo = (sq - hi.astype(F32)).astype(BF)
    return hi, lo


def attention_kernel(
    slots, starts, lens, x_ref, wqv_ref, wk_ref, gain_ref, wout_ref, wup_ref, wdown_ref, onehot_ref, far_ref,
    blockones_ref, out_ref, kaug, qbig, rows
):
    bands, flat, _ = x_ref.shape
    per_band = POOL // bands
    px = flat // per_band
    n2 = 2 * POOL
    lane = lax.broadcasted_iota(jnp.int32, (1, C), 1) // HEAD_DIM
    kaug[C:, :] = onehot_ref[...]
    for h in range(HEADS):
        qbig[h, :, C:] = far_ref[...]

    def pixel_pair(pp, carry):
        both = x_ref[:, pl.ds(pl.multiple_of(pp * 16, 16), 16), :].astype(F32)
        xa = both[:, :per_band].reshape(POOL, C)
        xb = both[:, per_band:].reshape(POOL, C)
        x = jnp.concatenate([xa, xb], axis=0)
        n = (x * lax.rsqrt(jnp.mean(x * x, axis=-1, keepdims=True) + EPS)).astype(BF)
        qv = jnp.dot(n, wqv_ref[...], preferred_element_type=F32).astype(BF)
        q = qv[:, :C].astype(F32)
        ss = jnp.dot(
            jnp.concatenate(square_parts(q), axis=1), blockones_ref[...], preferred_element_type=F32
        )
        q = q * lax.rsqrt(ss * (1.0 / HEAD_DIM) + EPS) * gain_ref[...]
        v = qv[:, C:]
        k = lax.dot_general(
            wk_ref[...], n, (((1,), (1,)), ((), ())), preferred_element_type=F32
        ).astype(BF)
        k = k.astype(F32).reshape(HEADS, HEAD_DIM, n2)
        ks = jnp.sum(k * k, axis=1, keepdims=True)
        kaug[:C, :] = (k * lax.rsqrt(ks * (1.0 / HEAD_DIM) + EPS)).reshape(C, n2).astype(BF)
        for h in range(HEADS):
            qbig[h, :, :C] = jnp.where(lane == h, q, 0.0).astype(BF)
        mixed = []
        for i in range(2):
            own = slice(i * POOL, (i + 1) * POOL)
            scores = jnp.dot(
                qbig[:, own, :].reshape(HEADS * POOL, 2 * C), kaug[:, own], preferred_element_type=F32
            )
            value_ones = jnp.concatenate([v[own], jnp.ones((POOL, C), BF)], axis=1)
            for h in range(HEADS):
                s = scores[h * POOL : (h + 1) * POOL]
                top = jnp.max(s, axis=-1, keepdims=True)
                e = jnp.exp2((s - top) * (LOG2E / 4)).astype(BF)
                o = jnp.dot(e, value_ones, preferred_element_type=F32)
                num = o[:, :C] if h == 0 else jnp.where(lane == h, o[:, :C], num)
                den = o[:, C:] if h == 0 else jnp.where(lane == h, o[:, C:], den)
            mixed.append((num / den).astype(BF))
        m = x + jnp.dot(
            jnp.concatenate(mixed, axis=0), wout_ref[...], preferred_element_type=F32
        )
        m = m.astype(BF).astype(F32)
        n = (m * lax.rsqrt(jnp.mean(m * m, axis=-1, keepdims=True) + EPS)).astype(BF)
        up = jnp.dot(n, wup_ref[...], preferred_element_type=F32) * 0.5
        up = (up + up * jnp.tanh(up)).astype(BF)
        res = m + jnp.dot(up, wdown_ref[...], preferred_element_type=F32)
        for i in range(2):
            rows[pl.ds(2 * pp + i, POOL, stride=px), :] = res[i * POOL : (i + 1) * POOL]
        return carry

    lax.fori_loop(0, px // 2, pixel_pair, 0)

    clips = out_ref.shape[1] // slots

    def hand_out(b, carry):
        parts = []
        for c in range(clips):
            for jj in range(slots):
                j = b * slots + jj
                frame = jnp.minimum(starts[c] + j, POOL - 1)
                part = rows[pl.ds(pl.multiple_of(frame * px, px), px), :]
                parts.append(jnp.where(j < lens[c], part, 0.0))
        out_ref[b] = jnp.stack(parts, axis=0).astype(BF)
        return carry

    lax.fori_loop(0, bands, hand_out, 0)


def attention(x, starts, lens, w_qkv, query_gain, w_out, w_up, w_down, slots):
    bands, flat, _ = x.shape
    px = flat // (POOL // bands)
    n2 = 2 * POOL
    clips = starts.shape[0]
    frame = jnp.arange(POOL, dtype=jnp.int32)
    clip_of = jnp.sum((frame[:, None] >= starts[None, :]).astype(jnp.int32), axis=1) - 1
    lane = jnp.arange(C, dtype=jnp.int32)
    onehot = (lane[:, None] == clip_of[None, :]).astype(BF)
    onehot = jnp.concatenate([onehot, onehot], axis=1)
    apart = jnp.where((lane[None, :] < clips) & (lane[None, :] != clip_of[:, None]), FAR, 0.0).astype(BF)
    apart = jnp.concatenate([apart, apart], axis=0)
    blockones = (lane[:, None] // HEAD_DIM == lane[None, :] // HEAD_DIM).astype(BF)
    blockones = jnp.concatenate([blockones, blockones], axis=0)
    wqv = jnp.concatenate([w_qkv[:, :C], w_qkv[:, 2 * C :]], axis=1)
    gain = query_gain.reshape(1, C)
    vmem = pl.BlockSpec(memory_space=pltpu.VMEM)
    smem = pl.BlockSpec(memory_space=pltpu.SMEM)
    return pl.pallas_call(
        functools.partial(attention_kernel, slots),
        out_shape=jax.ShapeDtypeStruct((bands, clips * slots, px, C), BF),
        in_specs=[smem, smem] + [vmem] * 10,
        out_specs=vmem,
        scratch_shapes=[
            pltpu.VMEM((2 * C, n2), BF),
            pltpu.VMEM((HEADS, n2, 2 * C), BF),
            pltpu.VMEM((POOL * px, C), F32),
        ],
        compiler_params=pltpu.CompilerParams(vmem_limit_bytes=48 * 2**20),
        cost_estimate=pl.CostEstimate(
            flops=2 * POOL * px * C * 4000, bytes_accessed=4 * 2**20, transcendentals=POOL * px * HEADS * KEYS
        ),
        name="pool_attention",
    )(starts, lens, x, wqv, w_qkv[:, C : 2 * C].T, gain, w_out, w_up, w_down, onehot, apart, blockones)


CHUNKS = 2


def rms_scale(values, reduce_axis):
    return values * lax.rsqrt(jnp.mean(values * values, axis=reduce_axis, keepdims=True) + EPS)


def conv_rows(latents, conv_weight, first, count):
    total = latents.shape[1]
    above, below = min(first, 1), min(total - first - count, 1)
    latent_wide = latents[:, first - above : first + count + below].astype(F32)
    normed = jax.nn.silu(rms_scale(latent_wide, -1)).astype(BF)
    convolved = lax.conv_general_dilated(
        normed,
        conv_weight,
        (1, 1),
        ((1 - above, 1 - below), (1, 1)),
        dimension_numbers=("NHWC", "HWIO", "NHWC"),
        preferred_element_type=F32,
    )
    return (latent_wide[:, above : above + count] + convolved).astype(BF)


def pack_kernel(slots, aims_of, clip_ref, y_ref, *out_refs):
    bands, _, px, _ = y_ref.shape
    for out_ref, aims in zip(out_refs, aims_of):
        for at, aim in enumerate(aims):
            c = clip_ref[aim]
            for jj in range(slots):
                part = y_ref[:, jnp.maximum(c, 0) * slots + jj].astype(F32)
                part = jnp.where(c >= 0, part, 0.0).reshape(bands * px, C)
                out_ref[at, jj] = part.astype(BF)


def pack(y, clip_of_aim, slots, aims_of):
    bands, _, px, _ = y.shape
    vmem = pl.BlockSpec(memory_space=pltpu.VMEM)
    return pl.pallas_call(
        functools.partial(pack_kernel, slots, aims_of),
        out_shape=[jax.ShapeDtypeStruct((len(aims), slots, bands * px, C), BF) for aims in aims_of],
        in_specs=[pl.BlockSpec(memory_space=pltpu.SMEM), vmem],
        out_specs=[vmem] * len(aims_of),
        compiler_params=pltpu.CompilerParams(vmem_limit_bytes=32 * 2**20),
        cost_estimate=pl.CostEstimate(flops=0, bytes_accessed=2 * 2**20, transcendentals=0),
        name="pack_slots",
    )(clip_of_aim, y)


def place_kernel(groups, slots, entries, me_ref, *refs):
    pieces, out_ref, sem = refs, refs[-2], refs[-1]
    chip, core = me_ref[0] // 2, lax.rem(me_ref[0], 2)
    copies = []
    for piece, at, chunk, hop, flip in entries:
        chunk_px = pieces[piece].shape[2]
        source = lax.rem(chip + groups // 2 - hop, groups // 2) * 2 + (1 - core if flip else core)
        for jj in range(slots):
            copies.append(
                pltpu.make_async_copy(
                    pieces[piece].at[at, jj],
                    out_ref.at[jj * groups + source, pl.ds(chunk * chunk_px, chunk_px)],
                    sem.at[len(copies)],
                )
            )
    for copy in copies:
        copy.start()
    for copy in copies:
        copy.wait()


def place(pieces, entries, me, groups, pixels, onto=None):
    slots = pieces[0].shape[1]
    vmem, anywhere = pl.BlockSpec(memory_space=pltpu.VMEM), pl.BlockSpec(memory_space=pl.ANY)
    more = [] if onto is None else [onto]
    return pl.pallas_call(
        functools.partial(place_kernel, groups, slots, entries),
        out_shape=jax.ShapeDtypeStruct((slots * groups, pixels, C), BF),
        in_specs=[pl.BlockSpec(memory_space=pltpu.SMEM)] + [vmem] * len(pieces) + [anywhere] * len(more),
        out_specs=anywhere,
        input_output_aliases={1 + len(pieces): 0} if more else {},
        scratch_shapes=[pltpu.SemaphoreType.DMA((len(entries) * slots,))],
        compiler_params=pltpu.CompilerParams(vmem_limit_bytes=32 * 2**20),
        cost_estimate=pl.CostEstimate(flops=0, bytes_accessed=3 * 2**20, transcendentals=0),
        name="place_slots",
    )(me[None], *pieces, *more)


def to_chip(value, hop, flip, groups):
    pairs = [
        (chip * 2 + core, (chip + hop) % (groups // 2) * 2 + (core ^ flip))
        for chip in range(groups // 2)
        for core in range(2)
    ]
    return lax.ppermute(value, "group", pairs) if hop or flip else value


def body(
    base_latents, clip_lengths, clip_group, conv_weight, w_qkv, query_gain, w_out, w_up, w_down
):
    groups = lax.axis_size("group")
    bands = lax.axis_size("band")
    frames_dev, tile_rows, tile_cols, channels = base_latents.shape
    pixels = tile_rows * tile_cols
    px = pixels // bands // CHUNKS
    chunk_rows = tile_rows // CHUNKS

    me = lax.axis_index("group")
    lengths = lax.dynamic_index_in_dim(clip_lengths, me, 0, keepdims=False)
    targets = lax.dynamic_index_in_dim(clip_group, me, 0, keepdims=False)
    starts = jnp.cumsum(lengths) - lengths
    slots = -(-LMAX // bands)
    chips = groups // 2
    aim_list = [(hop, flip) for hop in range(chips) for flip in range(2)]
    aims = jnp.stack(
        [lax.rem(me // 2 + hop, chips) * 2 + lax.rem(me + flip, 2) for hop, flip in aim_list]
    )
    hit = targets[None, :] == aims[:, None]
    clip_index = jnp.arange(targets.shape[0], dtype=jnp.int32)
    clip_of_aim = jnp.max(jnp.where(hit, clip_index[None, :], -1), axis=1)

    pieces, entries = [], []
    latents, to_swap = base_latents, []
    for chunk in range(CHUNKS):
        hidden = conv_rows(latents, conv_weight, chunk * chunk_rows, chunk_rows)
        latents, hidden = lax.optimization_barrier((latents, hidden))
        hidden = hidden.reshape(frames_dev, chunk_rows * tile_cols, channels).transpose(1, 0, 2)
        hidden = hidden.reshape(bands, px * frames_dev, channels)
        pencil = lax.all_to_all(hidden, "band", split_axis=0, concat_axis=0, tiled=True)
        refined = attention(pencil, starts, lengths, w_qkv, query_gain, w_out, w_up, w_down, slots)
        arrived = lax.all_to_all(refined, "band", split_axis=0, concat_axis=0, tiled=True)
        if chunk < CHUNKS - 1:
            packed = pack(
                arrived, clip_of_aim, slots, [[2 * hop, 2 * hop + 1] for hop in range(chips)]
            )
            for hop, slab in enumerate(packed):
                landed = to_chip(slab, hop, 0, groups)
                entries.append((len(pieces), 0, chunk, hop, 0))
                pieces.append(landed)
                to_swap.append((landed, chunk, hop))
        else:
            packed = pack(arrived, clip_of_aim, slots, [[i] for i in range(groups)])
            packed, landed = lax.optimization_barrier((packed, [slab for slab, _, _ in to_swap]))
            swapped = to_chip(jnp.stack([slab[1] for slab in landed]), 0, 1, groups)
            entries += [(len(pieces), at, of, hop, 1) for at, (_, of, hop) in enumerate(to_swap)]
            pieces.append(swapped)
            placed = place(pieces, entries, me, groups, pixels)
            pieces, entries = [], []
            for hop, flip in ((2, 0), (1, 0), (3, 0), (2, 1), (1, 1), (3, 1), (0, 1), (0, 0)):
                entries.append((len(pieces), 0, chunk, hop, flip))
                pieces.append(to_chip(packed[aim_list.index((hop, flip))], hop, flip, groups))
    placed = place(pieces, entries, me, groups, pixels, placed)
    return placed.reshape(1, slots * groups, tile_rows, tile_cols, channels)


def solution(mesh):
    placed = (P(("group", "band"), None, None, None), P(), P(), P(), P(), P(), P(), P(), P())
    return jax.shard_map(
        body,
        mesh=mesh,
        in_specs=placed,
        out_specs=P("group", "band", None, None, None),
        check_vma=False,
    )
```
